32 devices in a mesh: gz: 4 (over z), gy: 4 (over x, core), col: 2 (over y).
Axes of the slice: x: 2, y: 2, z: 4, core: 2. Of those that a mesh axis runs over, the one named last changes fastest.
Arguments:
- volume: bfloat16 [8, 8, 1024, 128], P('gz', 'gy', 'col'), may hold values from -6 to 6
- conv_weight: bfloat16 [27, 2, 1024, 1024], P(None, None, 'col'), may hold values from -0.0390625 to 0.0390625
- proj_weight: bfloat16 [1024, 512], replicated, may hold values from -0.1875 to 0.1875
Outputs:
- fine_tiles: float32 [32, 32, 4096], P('gz', 'gy', 'col')
The draws below stay inside these ranges and needn't reach their ends.
All inputs are finite; a program needn't handle non-finite values.
Results may differ from the reference program's by a relative error of at most 0.0029.
Values may be sent and summed in bfloat16 or wider, within the bound.
A program may use at most 128 MiB of HBM per device.

```python
import jax
import jax.numpy as jnp
from jax import lax

C = 1024
CO = 1024
F = 32
P_SIZE = 512
BX = 128
NZ = 8
NY = 8


def block_levels(own_key, extent, split, least, high):
    loudness, own = 1.0, jax.random.fold_in(own_key, 6)
    for dim, blocks in split:
        draws = jnp.exp(jax.random.uniform(jax.random.fold_in(own, dim), (blocks,), jnp.float32, least / len(split), high / len(split)))
        loudness = loudness * jnp.repeat(draws, extent[dim] // blocks).reshape([-1 if axis == dim else 1 for axis in range(len(extent))])
    return loudness


def centred(own_key, dims, scale, limit, pieces=(), kind=jnp.bfloat16):
    gain = block_levels(own_key, dims, pieces, -0.22, 0.18) if pieces else 1.0
    values = jax.random.normal(own_key, dims, jnp.float32) * scale * gain
    return jnp.minimum(jnp.maximum(values, -limit), limit).astype(kind)


def setup_inputs(seed: int = 0) -> dict:
    splits = jax.random.split(jax.random.key(seed), 4)
    volume = centred(splits[0], (NZ, NY, C, BX), 1.0, 6.0, ((0, 4), (1, 4), (2, 2)))
    conv_weight = centred(splits[1], (27, 2, CO, C), (27 * C) ** -0.5, 0.0390625, ((2, 2),))
    proj_weight = centred(splits[2], (CO, P_SIZE), CO ** -0.5, 0.1875)
    return dict(volume=volume, conv_weight=conv_weight, proj_weight=proj_weight)


def inverse_lift(low_band, high_band, along):
    length = low_band.shape[along]

    def window_of(array, first, last):
        return lax.slice_in_dim(array, first, last, axis=along)

    even_rows = window_of(low_band, 1, length - 1) - 0.25 * (window_of(high_band, 0, length - 2) + window_of(high_band, 1, length - 1))
    next_even = window_of(low_band, 2, length) - 0.25 * (window_of(high_band, 1, length - 1) + window_of(high_band, 2, length))
    odd_rows = window_of(high_band, 1, length - 1) + 0.5 * (even_rows + next_even)
    paired = jnp.stack([even_rows, odd_rows], axis=along + 1)
    new_shape = list(even_rows.shape)
    new_shape[along] = 2 * (length - 2)
    return paired.reshape(new_shape)


def synthesize(coefficients):
    quarter = coefficients.shape[-1] // 4
    bands = coefficients.reshape(coefficients.shape[:-1] + (4, quarter))
    low_z = inverse_lift(bands[..., 0, :], bands[..., 2, :], 0)
    high_z = inverse_lift(bands[..., 1, :], bands[..., 3, :], 0)
    return inverse_lift(low_z, high_z, 1)


def reference(volume, conv_weight, proj_weight):
    kernel = conv_weight.astype(jnp.float32).reshape((3, 3, 3, 2 * CO, C))
    conv_out = lax.conv_general_dilated(volume.astype(jnp.float32)[None], kernel, (1, 1, 1), ((1, 1), (1, 1), (1, 1)), dimension_numbers=("NDHCW", "DHWOI", "NDHCW"), precision=lax.Precision.HIGHEST)[0]
    gate_half = conv_out[:, :, :CO, :]
    values_half = conv_out[:, :, CO:, :]
    gated_values = (jax.nn.silu(gate_half) * values_half).astype(jnp.bfloat16)
    coefficients = jnp.einsum("zycx,cp->zyxp", gated_values.astype(jnp.float32), proj_weight.astype(jnp.float32), precision=lax.Precision.HIGHEST)
    padded = jnp.pad(coefficients, ((1, 1), (1, 1), (0, 0), (0, 0)), mode="wrap")
    middle = synthesize(padded)
    padded_middle = jnp.pad(middle, ((1, 1), (1, 1), (0, 0), (0, 0)), mode="wrap")
    fine_tiles = synthesize(padded_middle)
    return fine_tiles.reshape((4 * NZ, 4 * NY, BX * F))
```

```python
import functools

import jax
import jax.numpy as jnp
from jax import lax
from jax.experimental import pallas as pl
from jax.experimental.pallas import tpu as pltpu
from jax.sharding import PartitionSpec as P

MESH = pl.DeviceIdType.MESH
VMEM = pl.BlockSpec(memory_space=pltpu.VMEM)
AXES = ("gz", "gy", "col")


def place():
    return [lax.axis_index(a) for a in AXES], [lax.axis_size(a) for a in AXES]


def remote(src, dst, send, recv, target):
    return pltpu.make_async_remote_copy(
        src_ref=src, dst_ref=dst, send_sem=send, recv_sem=recv,
        device_id=target, device_id_type=MESH,
    )


def greet(target):
    pl.semaphore_signal(
        pltpu.get_barrier_semaphore(), inc=1, device_id=target, device_id_type=MESH
    )


def gather_kernel(vol, ext, own_sem, cs, cr, zs, zr, ys, yr):
    (gz, gy, col), (nz, ny, nc) = place()
    bz, by = vol.shape[:2]
    has_z = (gz > 0, gz < nz - 1)
    has_y = (gy > 0, gy < ny - 1)
    z_dev = ((gz - 1, gy, col), (gz + 1, gy, col))
    y_dev = ((gz, gy - 1, col), (gz, gy + 1, col))
    rows_z, rows_y = pl.ds(1, bz), pl.ds(1, by)

    own = pltpu.make_async_copy(vol, ext.at[rows_z, rows_y, col], own_sem)
    own.start()
    for j in range(1, nc):
        greet((gz, gy, lax.rem(col + j, nc)))
    count = nc - 1
    for d in range(2):
        pl.when(has_z[d])(functools.partial(greet, z_dev[d]))
        pl.when(has_y[d])(functools.partial(greet, y_dev[d]))
        count = count + has_z[d].astype(jnp.int32) + has_y[d].astype(jnp.int32)
    pl.semaphore_wait(pltpu.get_barrier_semaphore(), count)

    def col_copy(j, z, block, target):
        return remote(vol.at[z], ext.at[1 + z, rows_y, block], cs.at[j, z], cr.at[j, z], target)

    def z_copy(j, block, d):
        src, dst = ((1, bz + 1), (bz, 0))[d]
        return remote(
            ext.at[src, rows_y, block], ext.at[dst, rows_y, block],
            zs.at[j, d], zr.at[j, d], z_dev[d],
        )

    def y_copy(j, block, d, part):
        src, dst = ((1, by + 1), (by, 0))[d]
        z = (rows_z, pl.ds(0, 1), pl.ds(bz + 1, 1))[part]
        return remote(
            ext.at[z, src, block], ext.at[z, dst, block],
            ys.at[j, d, part], yr.at[j, d, part], y_dev[d],
        )

    for j in range(1, nc):
        for z in range(bz):
            col_copy(j, z, col, (gz, gy, lax.rem(col + j, nc))).start()

    for d in range(2):
        @pl.when(jnp.logical_not(has_z[d]))
        def _(d=d):
            ext[(0, bz + 1)[d]] = jnp.zeros(ext.shape[1:], ext.dtype)

        @pl.when(jnp.logical_not(has_y[d]))
        def _(d=d):
            for z in range(bz + 2):
                ext[z, (0, by + 1)[d]] = jnp.zeros(ext.shape[2:], ext.dtype)

    own.wait()
    blocks = [col] + [lax.rem(col + nc - j, nc) for j in range(1, nc)]
    for j, block in enumerate(blocks):
        order = [0] + [z for z in range(bz) if z > 0]
        for z in order:
            if j > 0:
                col_copy(j, z, block, (gz, gy, block)).wait_recv()
            if z == 0:
                pl.when(has_z[0])(lambda j=j, block=block: z_copy(j, block, 0).start())
            if z == bz - 1:
                pl.when(has_z[1])(lambda j=j, block=block: z_copy(j, block, 1).start())
        for d in range(2):
            pl.when(has_y[d])(lambda j=j, block=block, d=d: y_copy(j, block, d, 0).start())
    for j, block in enumerate(blocks):
        for h in range(2):
            @pl.when(has_z[h])
            def _(j=j, block=block, h=h):
                z_copy(j, block, 1 - h).wait_recv()
                for d in range(2):
                    pl.when(has_y[d])(lambda: y_copy(j, block, d, 1 + h).start())
    for j, block in enumerate(blocks):
        if j > 0:
            for z in range(bz):
                col_copy(j, z, block, (gz, gy, block)).wait_send()
        for d in range(2):
            pl.when(has_z[d])(lambda j=j, block=block, d=d: z_copy(j, block, d).wait_send())

            @pl.when(has_y[d])
            def _(j=j, block=block, d=d):
                y_copy(j, block, d, 0).wait_send()
                y_copy(j, block, 1 - d, 0).wait_recv()
                for h in range(2):
                    @pl.when(has_z[h])
                    def _(h=h):
                        y_copy(j, block, d, 1 + h).wait_send()
                        y_copy(j, block, 1 - d, 1 + h).wait_recv()


def gathered_brick(volume):
    bz, by, ch, bx = volume.shape
    nc = lax.axis_size("col")
    dma = pltpu.SemaphoreType.DMA
    return pl.pallas_call(
        gather_kernel,
        out_shape=jax.ShapeDtypeStruct((bz + 2, by + 2, nc, ch, bx), volume.dtype),
        in_specs=[pl.BlockSpec(memory_space=pl.ANY)],
        out_specs=VMEM,
        scratch_shapes=[
            dma, dma((nc, bz)), dma((nc, bz)), dma((nc, 2)), dma((nc, 2)),
            dma((nc, 2, 3)), dma((nc, 2, 3)),
        ],
        compiler_params=pltpu.CompilerParams(
            collective_id=0, has_side_effects=True, vmem_limit_bytes=32 << 20
        ),
        name="gather_brick",
    )(volume)


def conv_kernel(ext, weights, out, total):
    tap = pl.program_id(0)
    dz, dy, dx = tap // 9, lax.rem(tap // 3, 3), lax.rem(tap, 3)
    bz, by, bx, wide = out.shape
    channels = weights.shape[-1]
    matrix = weights[0].reshape(2 * wide, channels)
    for z in range(bz):
        cells = jnp.concatenate(
            [ext[dz + z, dy + y].reshape(channels, bx) for y in range(by)], axis=1
        )
        product = jnp.dot(matrix, cells, preferred_element_type=jnp.float32)

        @pl.when(tap < 3)
        def _():
            total[dx, z] = product

        @pl.when(tap >= 3)
        def _():
            total[dx, z] += product

    @pl.when(tap == pl.num_programs(0) - 1)
    def _():
        step = min(wide, 128)
        lane = lax.broadcasted_iota(jnp.int32, (step, bx), 1)

        def summed(z, first, y):
            rows, xs = pl.ds(first, step), pl.ds(y * bx, bx)
            before = pltpu.roll(total[0, z, rows, xs], 1, 1)
            after = pltpu.roll(total[2, z, rows, xs], bx - 1, 1)
            return (
                total[1, z, rows, xs]
                + jnp.where(lane == 0, 0.0, before)
                + jnp.where(lane == bx - 1, 0.0, after)
            )

        for z in range(bz):
            for y in range(by):
                for first in range(0, wide, step):
                    gate = summed(z, first, y)
                    value = summed(z, wide + first, y)
                    gated = gate / (1.0 + jnp.exp(-gate)) * value
                    out[z, y, :, pl.ds(first, step)] = gated.T.astype(out.dtype)


def gated_conv(ext, weights, brick):
    bz, by = brick
    taps, two, wide, channels = weights.shape
    bx = ext.shape[-1]
    return pl.pallas_call(
        conv_kernel,
        grid=(taps,),
        out_shape=jax.ShapeDtypeStruct((bz, by, bx, wide), jnp.bfloat16),
        in_specs=[
            pl.BlockSpec(ext.shape, lambda t: (0,) * 5),
            pl.BlockSpec((1, two, wide, channels), lambda t: (t, 0, 0, 0)),
        ],
        out_specs=pl.BlockSpec((bz, by, bx, wide), lambda t: (0,) * 4),
        scratch_shapes=[pltpu.VMEM((3, bz, two * wide, by * bx), jnp.float32)],
        compiler_params=pltpu.CompilerParams(vmem_limit_bytes=48 << 20),
        cost_estimate=pl.CostEstimate(
            flops=2 * taps * two * wide * channels * bz * by * bx,
            bytes_accessed=2 * weights.size + 2 * ext.size,
            transcendentals=bz * by * bx * wide,
        ),
        name="gated_conv",
    )(ext, weights)


def project_kernel(gated, proj, ext, other, rows, cs, cr, zs, zr, ys, yr):
    (gz, gy, col), (nz, ny, nc) = place()
    bz, by, bx, wide = gated.shape
    piece = bx // nc
    z_dev = ((lax.rem(gz + nz - 1, nz), gy, col), (lax.rem(gz + 1, nz), gy, col))
    y_dev = ((gz, lax.rem(gy + ny - 1, ny), col), (gz, lax.rem(gy + 1, ny), col))
    for j in range(1, nc):
        greet((gz, gy, lax.rem(col + j, nc)))
    for d in range(2):
        greet(z_dev[d])
        greet(y_dev[d])
    pl.semaphore_wait(pltpu.get_barrier_semaphore(), nc + 3)

    def col_copy(j):
        target = lax.rem(col + j, nc)
        xs = pl.ds(pl.multiple_of(target * piece, piece), piece)
        return remote(
            gated.at[:, :, xs], other.at[j], cs.at[j], cr.at[j], (gz, gy, target)
        )

    for j in range(1, nc):
        col_copy(j).start()

    def projected(cells, block):
        return jnp.dot(
            cells.reshape(bz * by * piece, wide),
            proj[pl.ds(pl.multiple_of(block * wide, wide), wide), :],
            preferred_element_type=jnp.float32,
        )

    total = projected(
        gated[:, :, pl.ds(pl.multiple_of(col * piece, piece), piece), :], col
    )
    for j in range(1, nc):
        col_copy(j).wait_recv()
        total += projected(other[j], lax.rem(col + nc - j, nc))

    bands, quads, lanes = 4, piece // 4, ext.shape[-1]
    for b in range(4):
        rows[b] = total[:, b * lanes : (b + 1) * lanes]
    width = lanes // 4
    slot = lax.broadcasted_iota(jnp.int32, (quads, lanes), 1) // width
    for z in range(bz):
        for y in range(by):
            first = (z * by + y) * piece
            for b in range(4):
                parts = [
                    rows[b, pl.ds(first + r, quads, stride=4), :]
                    for r in range(4)
                ]
                for q in range(bands):
                    packed = None
                    for r in range(4):
                        shift = ((r - q) * width) % lanes
                        part = pltpu.roll(parts[r], shift, 1) if shift else parts[r]
                        packed = part if packed is None else jnp.where(slot == r, part, packed)
                    ext[2 + z, 2 + y, b // 2, b % 2, q] = packed.astype(ext.dtype)

    def moves(n):
        return ((n, 0, True, 1), (n + 1, 1, False, 1), (2, n + 2, False, 0))

    def band(high):
        return pl.ds(1, 1) if high else pl.ds(0, 2)

    def z_copy(k):
        src, dst, high, d = moves(bz)[k]
        inner = pl.ds(2, by)
        return remote(
            ext.at[src, inner, band(high)], ext.at[dst, inner, band(high)],
            zs.at[k], zr.at[k], z_dev[d],
        )

    groups = ((2, bz, False), (0, 1, True), (1, 1, False), (bz + 2, 1, False))

    def y_copy(k, g):
        src, dst, high, d = moves(by)[k]
        start, size, z_high = groups[g]
        zr_ = pl.ds(start, size)
        return remote(
            ext.at[zr_, src, band(z_high), band(high)],
            ext.at[zr_, dst, band(z_high), band(high)],
            ys.at[k, g], yr.at[k, g], y_dev[d],
        )

    for k in (1, 2, 0):
        z_copy(k).start()
    for k in (1, 2, 0):
        y_copy(k, 0).start()
    for m in (1, 2, 0):
        z_copy(m).wait_recv()
        for k in (1, 2, 0):
            y_copy(k, m + 1).start()
    for j in range(1, nc):
        col_copy(j).wait_send()
    for k in range(3):
        z_copy(k).wait_send()
        for g in range(4):
            y_copy(k, g).wait_send()
    for k in range(3):
        for g in range(4):
            y_copy(k, g).wait_recv()


def projected_brick(gated, proj):
    bz, by, bx, wide = gated.shape
    nc = lax.axis_size("col")
    piece, lanes = bx // nc, proj.shape[1] // 4
    dma = pltpu.SemaphoreType.DMA
    return pl.pallas_call(
        project_kernel,
        out_shape=jax.ShapeDtypeStruct(
            (bz + 3, by + 3, 2, 2, 4, piece // 4, lanes), jnp.bfloat16
        ),
        in_specs=[VMEM, VMEM],
        out_specs=VMEM,
        scratch_shapes=[
            pltpu.VMEM((nc, bz, by, piece, wide), gated.dtype),
            pltpu.VMEM((4, bz * by * piece, lanes), jnp.float32),
            dma((nc,)), dma((nc,)), dma((3,)), dma((3,)), dma((3, 4)), dma((3, 4)),
        ],
        compiler_params=pltpu.CompilerParams(
            collective_id=1, has_side_effects=True, vmem_limit_bytes=32 << 20
        ),
        name="project",
    )(gated, proj)


def coarse_lift(low, high):
    count = len(high)
    even = [low[i] - 0.25 * (high[i - 1] + high[i]) for i in range(1, count)]
    odd = [high[i + 1] + 0.5 * (even[i] + even[i + 1]) for i in range(count - 2)]
    result = []
    for i in range(count - 2):
        result += [odd[i], even[i + 1]]
    return result


def fine_lift(low, high):
    count = len(high)
    even = [low[i] - 0.25 * (high[i - 1] + high[i]) for i in range(1, count)]
    result = []
    for i in range(count - 2):
        result += [even[i], high[i + 1] + 0.5 * (even[i] + even[i + 1])]
    return result


def synthesis_kernel(ext, out, middle, tiles):
    nz, ny = ext.shape[:2]
    for band in range(4):
        def column(y, hz, hy):
            return [
                None if z == 0 and not hz else ext[z, y, hz, hy, band].astype(jnp.float32)
                for z in range(nz)
            ]

        low = [
            None if y == 0 else coarse_lift(column(y, 0, 0), column(y, 1, 0))
            for y in range(ny)
        ]
        high = [coarse_lift(column(y, 0, 1), column(y, 1, 1)) for y in range(ny)]
        for z in range(len(high[0])):
            line = coarse_lift(
                [None if part is None else part[z] for part in low],
                [part[z] for part in high],
            )
            for y, cells in enumerate(line):
                middle[band, z, y] = cells
    mz, my = middle.shape[1:3]
    low, high = [], []
    for y in range(my):
        low.append(fine_lift([middle[0, z, y] for z in range(mz)], [middle[2, z, y] for z in range(mz)]))
        high.append(fine_lift([middle[1, z, y] for z in range(mz)], [middle[3, z, y] for z in range(mz)]))
    quads, lanes = middle.shape[3:]
    for z in range(out.shape[0]):
        line = fine_lift([part[z] for part in low], [part[z] for part in high])
        for y, cells in enumerate(line):
            tiles[z, pl.ds(y * quads, quads), :] = cells
        for quad in range(quads):
            out[z, :, pl.ds(quad * lanes, lanes)] = tiles[z, pl.ds(quad, out.shape[1], stride=quads), :]


def synthesized(ext):
    nz, ny = ext.shape[:2]
    quads, lanes = ext.shape[-2:]
    fz, fy = 4 * (nz - 3), 4 * (ny - 3)
    return pl.pallas_call(
        synthesis_kernel,
        out_shape=jax.ShapeDtypeStruct((fz, fy, quads * lanes), jnp.float32),
        in_specs=[VMEM],
        out_specs=VMEM,
        scratch_shapes=[
            pltpu.VMEM((4, 2 * (nz - 2), 2 * (ny - 2), quads, lanes), jnp.float32),
            pltpu.VMEM((fz, fy * quads, lanes), jnp.float32),
        ],
        compiler_params=pltpu.CompilerParams(vmem_limit_bytes=32 << 20),
        name="synthesis",
    )(ext)


def on_device_kernels(volume, conv_weight, proj_weight):
    ext = gathered_brick(volume)
    gated = gated_conv(ext, conv_weight, volume.shape[:2])
    return synthesized(projected_brick(gated, proj_weight))


def fits(volume, conv_weight, proj_weight):
    bz, by, ch, bx = volume.shape
    wide, piece = conv_weight.shape[2], bx // lax.axis_size("col")
    return (
        min(bz, by) >= 2
        and min(lax.axis_size("gz"), lax.axis_size("gy")) >= 3
        and ch % 16 == 0 and bx == 128 and wide % 128 == 0
        and piece % 64 == 0 and proj_weight.shape[1] == 4 * 128
    )


def extended_2(cells, sides, width, closed):
    for axis, dim in sides:
        count = lax.axis_size(axis)
        ends = count if closed else count - 1
        head = lax.slice_in_dim(cells, 0, width, axis=dim)
        tail = lax.slice_in_dim(cells, cells.shape[dim] - width, cells.shape[dim], axis=dim)
        cells = jnp.concatenate(
            [
                lax.ppermute(tail, axis, [(i, (i + 1) % count) for i in range(ends)]),
                cells,
                lax.ppermute(head, axis, [((i + 1) % count, i) for i in range(ends)]),
            ],
            axis=dim,
        )
    return cells


def inverse_lift(low_band, high_band, along):
    length = low_band.shape[along]

    def window_of(array, first, last):
        return lax.slice_in_dim(array, first, last, axis=along)

    even_rows = window_of(low_band, 1, length - 1) - 0.25 * (
        window_of(high_band, 0, length - 2) + window_of(high_band, 1, length - 1)
    )
    next_even = window_of(low_band, 2, length) - 0.25 * (
        window_of(high_band, 1, length - 1) + window_of(high_band, 2, length)
    )
    odd_rows = window_of(high_band, 1, length - 1) + 0.5 * (even_rows + next_even)
    paired = jnp.stack([even_rows, odd_rows], axis=along + 1)
    new_shape = list(even_rows.shape)
    new_shape[along] = 2 * (length - 2)
    return paired.reshape(new_shape)


def synthesize(coefficients):
    quarter = coefficients.shape[-1] // 4
    bands = coefficients.reshape(coefficients.shape[:-1] + (4, quarter))
    low_z = inverse_lift(bands[..., 0, :], bands[..., 2, :], 0)
    high_z = inverse_lift(bands[..., 1, :], bands[..., 3, :], 0)
    return inverse_lift(low_z, high_z, 1)


def convolve(brick_data, tap_weights):
    kernel = tap_weights.reshape(
        (3, 3, 3, tap_weights.shape[1] * tap_weights.shape[2], tap_weights.shape[3])
    )
    result = lax.conv_general_dilated(
        brick_data[None],
        kernel,
        (1, 1, 1),
        ((0, 0), (0, 0), (1, 1)),
        dimension_numbers=("NDHCW", "DHWOI", "NDHCW"),
        preferred_element_type=jnp.float32,
    )
    return result[0]


def on_device(volume, conv_weight, proj_weight):
    if fits(volume, conv_weight, proj_weight):
        return on_device_kernels(volume, conv_weight, proj_weight)
    out_width = conv_weight.shape[2]
    gathered = lax.all_gather(volume, "col", axis=2, tiled=True)
    extended = extended_2(gathered, (("gz", 0), ("gy", 1)), 1, False)
    conv_out = convolve(extended, conv_weight)
    gated_values = (
        jax.nn.silu(conv_out[:, :, :out_width, :]) * conv_out[:, :, out_width:, :]
    ).astype(jnp.bfloat16)
    coefficients = jnp.einsum(
        "zycx,cp->zyxp",
        lax.all_to_all(gated_values, "col", split_axis=3, concat_axis=2, tiled=True),
        proj_weight,
        preferred_element_type=jnp.float32,
    )
    coarse = extended_2(coefficients, (("gz", 0), ("gy", 1)), 1, True)
    middle = synthesize(coarse)
    middle_rims = extended_2(middle, (("gz", 0), ("gy", 1)), 1, True)
    fine_tiles = synthesize(middle_rims)
    return fine_tiles.reshape(
        (fine_tiles.shape[0], fine_tiles.shape[1], fine_tiles.shape[2] * fine_tiles.shape[3])
    )


def solution(mesh):
    return jax.shard_map(
        on_device,
        mesh=mesh,
        in_specs=(P("gz", "gy", "col", None), P(None, None, "col", None), P()),
        out_specs=P("gz", "gy", "col"),
        check_vma=False,
    )
```

```python
import functools

import jax
import jax.numpy as jnp
from jax import lax
from jax.experimental import pallas as pl
from jax.experimental.pallas import tpu as pltpu
from jax.sharding import PartitionSpec as P

MESH = pl.DeviceIdType.MESH
VMEM = pl.BlockSpec(memory_space=pltpu.VMEM)
AXES = ("gz", "gy", "col")


def place():
    return [lax.axis_index(a) for a in AXES], [lax.axis_size(a) for a in AXES]


def remote(src, dst, send, recv, target):
    return pltpu.make_async_remote_copy(
        src_ref=src, dst_ref=dst, send_sem=send, recv_sem=recv,
        device_id=target, device_id_type=MESH,
    )


def greet(target):
    pl.semaphore_signal(
        pltpu.get_barrier_semaphore(), inc=1, device_id=target, device_id_type=MESH
    )


def gather_kernel(vol, ext, own_sem, cs, cr, zs, zr, ys, yr):
    (gz, gy, col), (nz, ny, nc) = place()
    bz, by = vol.shape[:2]
    has_z = (gz > 0, gz < nz - 1)
    has_y = (gy > 0, gy < ny - 1)
    z_dev = ((gz - 1, gy, col), (gz + 1, gy, col))
    y_dev = ((gz, gy - 1, col), (gz, gy + 1, col))
    rows_z, rows_y = pl.ds(1, bz), pl.ds(1, by)

    own = pltpu.make_async_copy(vol, ext.at[rows_z, rows_y, col], own_sem)
    own.start()
    for j in range(1, nc):
        greet((gz, gy, lax.rem(col + j, nc)))
    count = nc - 1
    for d in range(2):
        pl.when(has_z[d])(functools.partial(greet, z_dev[d]))
        pl.when(has_y[d])(functools.partial(greet, y_dev[d]))
        count = count + has_z[d].astype(jnp.int32) + has_y[d].astype(jnp.int32)
    pl.semaphore_wait(pltpu.get_barrier_semaphore(), count)

    def col_copy(j, z, block, target):
        return remote(vol.at[z], ext.at[1 + z, rows_y, block], cs.at[j, z], cr.at[j, z], target)

    def z_copy(j, block, d):
        src, dst = ((1, bz + 1), (bz, 0))[d]
        return remote(
            ext.at[src, rows_y, block], ext.at[dst, rows_y, block],
            zs.at[j, d], zr.at[j, d], z_dev[d],
        )

    def y_copy(j, block, d, part):
        src, dst = ((1, by + 1), (by, 0))[d]
        z = (rows_z, pl.ds(0, 1), pl.ds(bz + 1, 1))[part]
        return remote(
            ext.at[z, src, block], ext.at[z, dst, block],
            ys.at[j, d, part], yr.at[j, d, part], y_dev[d],
        )

    for j in range(1, nc):
        for z in range(bz):
            col_copy(j, z, col, (gz, gy, lax.rem(col + j, nc))).start()

    for d in range(2):
        @pl.when(jnp.logical_not(has_z[d]))
        def _(d=d):
            ext[(0, bz + 1)[d]] = jnp.zeros(ext.shape[1:], ext.dtype)

        @pl.when(jnp.logical_not(has_y[d]))
        def _(d=d):
            for z in range(bz + 2):
                ext[z, (0, by + 1)[d]] = jnp.zeros(ext.shape[2:], ext.dtype)

    own.wait()
    blocks = [col] + [lax.rem(col + nc - j, nc) for j in range(1, nc)]
    for j, block in enumerate(blocks):
        order = [0] + [z for z in range(bz) if z > 0]
        for z in order:
            if j > 0:
                col_copy(j, z, block, (gz, gy, block)).wait_recv()
            if z == 0:
                pl.when(has_z[0])(lambda j=j, block=block: z_copy(j, block, 0).start())
            if z == bz - 1:
                pl.when(has_z[1])(lambda j=j, block=block: z_copy(j, block, 1).start())
        for d in range(2):
            pl.when(has_y[d])(lambda j=j, block=block, d=d: y_copy(j, block, d, 0).start())
    for j, block in enumerate(blocks):
        for h in range(2):
            @pl.when(has_z[h])
            def _(j=j, block=block, h=h):
                z_copy(j, block, 1 - h).wait_recv()
                for d in range(2):
                    pl.when(has_y[d])(lambda: y_copy(j, block, d, 1 + h).start())
    for j, block in enumerate(blocks):
        if j > 0:
            for z in range(bz):
                col_copy(j, z, block, (gz, gy, block)).wait_send()
        for d in range(2):
            pl.when(has_z[d])(lambda j=j, block=block, d=d: z_copy(j, block, d).wait_send())

            @pl.when(has_y[d])
            def _(j=j, block=block, d=d):
                y_copy(j, block, d, 0).wait_send()
                y_copy(j, block, 1 - d, 0).wait_recv()
                for h in range(2):
                    @pl.when(has_z[h])
                    def _(h=h):
                        y_copy(j, block, d, 1 + h).wait_send()
                        y_copy(j, block, 1 - d, 1 + h).wait_recv()


def gathered_brick(volume):
    bz, by, ch, bx = volume.shape
    nc = lax.axis_size("col")
    dma = pltpu.SemaphoreType.DMA
    return pl.pallas_call(
        gather_kernel,
        out_shape=jax.ShapeDtypeStruct((bz + 2, by + 2, nc, ch, bx), volume.dtype),
        in_specs=[pl.BlockSpec(memory_space=pl.ANY)],
        out_specs=VMEM,
        scratch_shapes=[
            dma, dma((nc, bz)), dma((nc, bz)), dma((nc, 2)), dma((nc, 2)),
            dma((nc, 2, 3)), dma((nc, 2, 3)),
        ],
        compiler_params=pltpu.CompilerParams(
            collective_id=0, has_side_effects=True, vmem_limit_bytes=32 << 20
        ),
        name="gather_brick",
    )(volume)


def conv_kernel(ext, weights, out, total):
    step_index = pl.program_id(0)
    dz, dx = step_index // 3, lax.rem(step_index, 3)
    bz, by, bx, wide = out.shape
    channels = weights.shape[-1]

    @pl.when(dz == 0)
    def _():
        total[dx] = jnp.zeros(total.shape[1:], total.dtype)

    for dy in range(3):
        cells = jnp.concatenate(
            [
                ext[dz + z, dy + y].reshape(channels, bx)
                for z in range(bz)
                for y in range(by)
            ],
            axis=1,
        )
        matrix = weights[0, dy, 0].reshape(2 * wide, channels)
        total[dx] += jnp.dot(matrix, cells, preferred_element_type=jnp.float32)

    @pl.when(step_index == pl.num_programs(0) - 1)
    def _():
        step = min(wide, 128)
        lane = lax.broadcasted_iota(jnp.int32, (step, bx), 1)

        def summed(z, first, y):
            rows, xs = pl.ds(first, step), pl.ds((z * by + y) * bx, bx)
            before = pltpu.roll(total[0, rows, xs], 1, 1)
            after = pltpu.roll(total[2, rows, xs], bx - 1, 1)
            return (
                total[1, rows, xs]
                + jnp.where(lane == 0, 0.0, before)
                + jnp.where(lane == bx - 1, 0.0, after)
            )

        for z in range(bz):
            for y in range(by):
                for first in range(0, wide, step):
                    gate = summed(z, first, y)
                    value = summed(z, wide + first, y)
                    gated = gate / (1.0 + jnp.exp(-gate)) * value
                    out[z, y, :, pl.ds(first, step)] = gated.T.astype(out.dtype)


def gated_conv(ext, weights, brick):
    bz, by = brick
    taps, two, wide, channels = weights.shape
    bx = ext.shape[-1]
    return pl.pallas_call(
        conv_kernel,
        grid=(9,),
        out_shape=jax.ShapeDtypeStruct((bz, by, bx, wide), jnp.bfloat16),
        in_specs=[
            pl.BlockSpec(ext.shape, lambda t: (0,) * 5),
            pl.BlockSpec(
                (1, 3, 1, two, wide, channels), lambda t: (t // 3, 0, t % 3, 0, 0, 0)
            ),
        ],
        out_specs=pl.BlockSpec((bz, by, bx, wide), lambda t: (0,) * 4),
        scratch_shapes=[pltpu.VMEM((3, two * wide, bz * by * bx), jnp.float32)],
        compiler_params=pltpu.CompilerParams(vmem_limit_bytes=48 << 20),
        cost_estimate=pl.CostEstimate(
            flops=2 * taps * two * wide * channels * bz * by * bx,
            bytes_accessed=2 * weights.size + 2 * ext.size,
            transcendentals=bz * by * bx * wide,
        ),
        name="gated_conv",
    )(ext, weights.reshape((3, 3, 3) + weights.shape[1:]))


def project_kernel(gated, proj, ext, other, rows, cs, cr, zs, zr, ys, yr):
    (gz, gy, col), (nz, ny, nc) = place()
    bz, by, bx, wide = gated.shape
    piece = bx // nc
    z_dev = ((lax.rem(gz + nz - 1, nz), gy, col), (lax.rem(gz + 1, nz), gy, col))
    y_dev = ((gz, lax.rem(gy + ny - 1, ny), col), (gz, lax.rem(gy + 1, ny), col))
    for j in range(1, nc):
        greet((gz, gy, lax.rem(col + j, nc)))
    for d in range(2):
        greet(z_dev[d])
        greet(y_dev[d])
    pl.semaphore_wait(pltpu.get_barrier_semaphore(), nc + 3)

    def col_copy(j):
        target = lax.rem(col + j, nc)
        xs = pl.ds(pl.multiple_of(target * piece, piece), piece)
        return remote(
            gated.at[:, :, xs], other.at[j], cs.at[j], cr.at[j], (gz, gy, target)
        )

    for j in range(1, nc):
        col_copy(j).start()

    def projected(cells, block):
        return jnp.dot(
            cells.reshape(bz * by * piece, wide),
            proj[pl.ds(pl.multiple_of(block * wide, wide), wide), :],
            preferred_element_type=jnp.float32,
        )

    total = projected(
        gated[:, :, pl.ds(pl.multiple_of(col * piece, piece), piece), :], col
    )
    for j in range(1, nc):
        col_copy(j).wait_recv()
        total += projected(other[j], lax.rem(col + nc - j, nc))

    bands, quads, lanes = 4, piece // 4, ext.shape[-1]
    for b in range(4):
        rows[b] = total[:, b * lanes : (b + 1) * lanes]
    width = lanes // 4
    slot = lax.broadcasted_iota(jnp.int32, (quads, lanes), 1) // width
    for z in range(bz):
        for y in range(by):
            first = (z * by + y) * piece
            for b in range(4):
                parts = [
                    rows[b, pl.ds(first + r, quads, stride=4), :]
                    for r in range(4)
                ]
                for q in range(bands):
                    packed = None
                    for r in range(4):
                        shift = ((r - q) * width) % lanes
                        part = pltpu.roll(parts[r], shift, 1) if shift else parts[r]
                        packed = part if packed is None else jnp.where(slot == r, part, packed)
                    ext[2 + z, 2 + y, b // 2, b % 2, q] = packed.astype(ext.dtype)

    def moves(n):
        return ((n, 0, True, 1), (n + 1, 1, False, 1), (2, n + 2, False, 0))

    def band(high):
        return pl.ds(1, 1) if high else pl.ds(0, 2)

    def z_copy(k):
        src, dst, high, d = moves(bz)[k]
        inner = pl.ds(2, by)
        return remote(
            ext.at[src, inner, band(high)], ext.at[dst, inner, band(high)],
            zs.at[k], zr.at[k], z_dev[d],
        )

    groups = ((2, bz, False), (0, 1, True), (1, 1, False), (bz + 2, 1, False))

    def y_copy(k, g):
        src, dst, high, d = moves(by)[k]
        start, size, z_high = groups[g]
        zr_ = pl.ds(start, size)
        return remote(
            ext.at[zr_, src, band(z_high), band(high)],
            ext.at[zr_, dst, band(z_high), band(high)],
            ys.at[k, g], yr.at[k, g], y_dev[d],
        )

    for k in (1, 2, 0):
        z_copy(k).start()
    for k in (1, 2, 0):
        y_copy(k, 0).start()
    for m in (1, 2, 0):
        z_copy(m).wait_recv()
        for k in (1, 2, 0):
            y_copy(k, m + 1).start()
    for j in range(1, nc):
        col_copy(j).wait_send()
    for k in range(3):
        z_copy(k).wait_send()
        for g in range(4):
            y_copy(k, g).wait_send()
    for k in range(3):
        for g in range(4):
            y_copy(k, g).wait_recv()


def projected_brick(gated, proj):
    bz, by, bx, wide = gated.shape
    nc = lax.axis_size("col")
    piece, lanes = bx // nc, proj.shape[1] // 4
    dma = pltpu.SemaphoreType.DMA
    return pl.pallas_call(
        project_kernel,
        out_shape=jax.ShapeDtypeStruct(
            (bz + 3, by + 3, 2, 2, 4, piece // 4, lanes), jnp.bfloat16
        ),
        in_specs=[VMEM, VMEM],
        out_specs=VMEM,
        scratch_shapes=[
            pltpu.VMEM((nc, bz, by, piece, wide), gated.dtype),
            pltpu.VMEM((4, bz * by * piece, lanes), jnp.float32),
            dma((nc,)), dma((nc,)), dma((3,)), dma((3,)), dma((3, 4)), dma((3, 4)),
        ],
        compiler_params=pltpu.CompilerParams(
            collective_id=1, has_side_effects=True, vmem_limit_bytes=32 << 20
        ),
        name="project",
    )(gated, proj)


def coarse_lift(low, high):
    count = len(high)
    even = [low[i] - 0.25 * (high[i - 1] + high[i]) for i in range(1, count)]
    odd = [high[i + 1] + 0.5 * (even[i] + even[i + 1]) for i in range(count - 2)]
    result = []
    for i in range(count - 2):
        result += [odd[i], even[i + 1]]
    return result


def fine_lift(low, high):
    count = len(high)
    even = [low[i] - 0.25 * (high[i - 1] + high[i]) for i in range(1, count)]
    result = []
    for i in range(count - 2):
        result += [even[i], high[i + 1] + 0.5 * (even[i] + even[i + 1])]
    return result


def synthesis_kernel(ext, out, middle, tiles):
    nz, ny = ext.shape[:2]
    for band in range(4):
        def column(y, hz, hy):
            return [
                None if z == 0 and not hz else ext[z, y, hz, hy, band].astype(jnp.float32)
                for z in range(nz)
            ]

        low = [
            None if y == 0 else coarse_lift(column(y, 0, 0), column(y, 1, 0))
            for y in range(ny)
        ]
        high = [coarse_lift(column(y, 0, 1), column(y, 1, 1)) for y in range(ny)]
        for z in range(len(high[0])):
            line = coarse_lift(
                [None if part is None else part[z] for part in low],
                [part[z] for part in high],
            )
            for y, cells in enumerate(line):
                middle[band, z, y] = cells
    mz, my = middle.shape[1:3]
    low, high = [], []
    for y in range(my):
        low.append(fine_lift([middle[0, z, y] for z in range(mz)], [middle[2, z, y] for z in range(mz)]))
        high.append(fine_lift([middle[1, z, y] for z in range(mz)], [middle[3, z, y] for z in range(mz)]))
    quads, lanes = middle.shape[3:]
    for z in range(out.shape[0]):
        line = fine_lift([part[z] for part in low], [part[z] for part in high])
        for y, cells in enumerate(line):
            tiles[z, pl.ds(y * quads, quads), :] = cells
        for quad in range(quads):
            out[z, :, pl.ds(quad * lanes, lanes)] = tiles[z, pl.ds(quad, out.shape[1], stride=quads), :]


def synthesized(ext):
    nz, ny = ext.shape[:2]
    quads, lanes = ext.shape[-2:]
    fz, fy = 4 * (nz - 3), 4 * (ny - 3)
    return pl.pallas_call(
        synthesis_kernel,
        out_shape=jax.ShapeDtypeStruct((fz, fy, quads * lanes), jnp.float32),
        in_specs=[VMEM],
        out_specs=VMEM,
        scratch_shapes=[
            pltpu.VMEM((4, 2 * (nz - 2), 2 * (ny - 2), quads, lanes), jnp.float32),
            pltpu.VMEM((fz, fy * quads, lanes), jnp.float32),
        ],
        compiler_params=pltpu.CompilerParams(vmem_limit_bytes=32 << 20),
        name="synthesis",
    )(ext)


def on_device_kernels(volume, conv_weight, proj_weight):
    ext = gathered_brick(volume)
    gated = gated_conv(ext, conv_weight, volume.shape[:2])
    return synthesized(projected_brick(gated, proj_weight))


def fits(volume, conv_weight, proj_weight):
    bz, by, ch, bx = volume.shape
    wide, piece = conv_weight.shape[2], bx // lax.axis_size("col")
    return (
        min(bz, by) >= 2
        and min(lax.axis_size("gz"), lax.axis_size("gy")) >= 3
        and ch % 16 == 0 and bx == 128 and wide % 128 == 0
        and piece % 64 == 0 and proj_weight.shape[1] == 4 * 128
    )


def extended_2(cells, sides, width, closed):
    for axis, dim in sides:
        count = lax.axis_size(axis)
        ends = count if closed else count - 1
        head = lax.slice_in_dim(cells, 0, width, axis=dim)
        tail = lax.slice_in_dim(cells, cells.shape[dim] - width, cells.shape[dim], axis=dim)
        cells = jnp.concatenate(
            [
                lax.ppermute(tail, axis, [(i, (i + 1) % count) for i in range(ends)]),
                cells,
                lax.ppermute(head, axis, [((i + 1) % count, i) for i in range(ends)]),
            ],
            axis=dim,
        )
    return cells


def inverse_lift(low_band, high_band, along):
    length = low_band.shape[along]

    def window_of(array, first, last):
        return lax.slice_in_dim(array, first, last, axis=along)

    even_rows = window_of(low_band, 1, length - 1) - 0.25 * (
        window_of(high_band, 0, length - 2) + window_of(high_band, 1, length - 1)
    )
    next_even = window_of(low_band, 2, length) - 0.25 * (
        window_of(high_band, 1, length - 1) + window_of(high_band, 2, length)
    )
    odd_rows = window_of(high_band, 1, length - 1) + 0.5 * (even_rows + next_even)
    paired = jnp.stack([even_rows, odd_rows], axis=along + 1)
    new_shape = list(even_rows.shape)
    new_shape[along] = 2 * (length - 2)
    return paired.reshape(new_shape)


def synthesize(coefficients):
    quarter = coefficients.shape[-1] // 4
    bands = coefficients.reshape(coefficients.shape[:-1] + (4, quarter))
    low_z = inverse_lift(bands[..., 0, :], bands[..., 2, :], 0)
    high_z = inverse_lift(bands[..., 1, :], bands[..., 3, :], 0)
    return inverse_lift(low_z, high_z, 1)


def convolve(brick_data, tap_weights):
    kernel = tap_weights.reshape(
        (3, 3, 3, tap_weights.shape[1] * tap_weights.shape[2], tap_weights.shape[3])
    )
    result = lax.conv_general_dilated(
        brick_data[None],
        kernel,
        (1, 1, 1),
        ((0, 0), (0, 0), (1, 1)),
        dimension_numbers=("NDHCW", "DHWOI", "NDHCW"),
        preferred_element_type=jnp.float32,
    )
    return result[0]


def on_device(volume, conv_weight, proj_weight):
    if fits(volume, conv_weight, proj_weight):
        return on_device_kernels(volume, conv_weight, proj_weight)
    out_width = conv_weight.shape[2]
    gathered = lax.all_gather(volume, "col", axis=2, tiled=True)
    extended = extended_2(gathered, (("gz", 0), ("gy", 1)), 1, False)
    conv_out = convolve(extended, conv_weight)
    gated_values = (
        jax.nn.silu(conv_out[:, :, :out_width, :]) * conv_out[:, :, out_width:, :]
    ).astype(jnp.bfloat16)
    coefficients = jnp.einsum(
        "zycx,cp->zyxp",
        lax.all_to_all(gated_values, "col", split_axis=3, concat_axis=2, tiled=True),
        proj_weight,
        preferred_element_type=jnp.float32,
    )
    coarse = extended_2(coefficients, (("gz", 0), ("gy", 1)), 1, True)
    middle = synthesize(coarse)
    middle_rims = extended_2(middle, (("gz", 0), ("gy", 1)), 1, True)
    fine_tiles = synthesize(middle_rims)
    return fine_tiles.reshape(
        (fine_tiles.shape[0], fine_tiles.shape[1], fine_tiles.shape[2] * fine_tiles.shape[3])
    )


def solution(mesh):
    return jax.shard_map(
        on_device,
        mesh=mesh,
        in_specs=(P("gz", "gy", "col", None), P(None, None, "col", None), P()),
        out_specs=P("gz", "gy", "col"),
        check_vma=False,
    )
```

```python
import functools

import jax
import jax.numpy as jnp
from jax import lax
from jax.experimental import pallas as pl
from jax.experimental.pallas import tpu as pltpu
from jax.sharding import PartitionSpec as P

MESH = pl.DeviceIdType.MESH
VMEM = pl.BlockSpec(memory_space=pltpu.VMEM)
AXES = ("gz", "gy", "col")


def place():
    return [lax.axis_index(a) for a in AXES], [lax.axis_size(a) for a in AXES]


def remote(src, dst, send, recv, target):
    return pltpu.make_async_remote_copy(
        src_ref=src, dst_ref=dst, send_sem=send, recv_sem=recv,
        device_id=target, device_id_type=MESH,
    )


def greet(target):
    pl.semaphore_signal(
        pltpu.get_barrier_semaphore(), inc=1, device_id=target, device_id_type=MESH
    )


def gather_kernel(vol, ext, own_sem, cs, cr, zs, zr, ys, yr):
    (gz, gy, col), (nz, ny, nc) = place()
    bz, by = vol.shape[:2]
    has_z = (gz > 0, gz < nz - 1)
    has_y = (gy > 0, gy < ny - 1)
    z_dev = ((gz - 1, gy, col), (gz + 1, gy, col))
    y_dev = ((gz, gy - 1, col), (gz, gy + 1, col))
    rows_z, rows_y = pl.ds(1, bz), pl.ds(1, by)

    own = pltpu.make_async_copy(vol, ext.at[rows_z, rows_y, col], own_sem)
    own.start()
    for j in range(1, nc):
        greet((gz, gy, lax.rem(col + j, nc)))
    count = nc - 1
    for d in range(2):
        pl.when(has_z[d])(functools.partial(greet, z_dev[d]))
        pl.when(has_y[d])(functools.partial(greet, y_dev[d]))
        count = count + has_z[d].astype(jnp.int32) + has_y[d].astype(jnp.int32)
    pl.semaphore_wait(pltpu.get_barrier_semaphore(), count)

    def col_copy(j, z, block, target):
        return remote(vol.at[z], ext.at[1 + z, rows_y, block], cs.at[j, z], cr.at[j, z], target)

    def z_copy(j, block, d):
        src, dst = ((1, bz + 1), (bz, 0))[d]
        return remote(
            ext.at[src, rows_y, block], ext.at[dst, rows_y, block],
            zs.at[j, d], zr.at[j, d], z_dev[d],
        )

    def y_copy(j, block, d, part):
        src, dst = ((1, by + 1), (by, 0))[d]
        z = (rows_z, pl.ds(0, 1), pl.ds(bz + 1, 1))[part]
        return remote(
            ext.at[z, src, block], ext.at[z, dst, block],
            ys.at[j, d, part], yr.at[j, d, part], y_dev[d],
        )

    for j in range(1, nc):
        for z in range(bz):
            col_copy(j, z, col, (gz, gy, lax.rem(col + j, nc))).start()

    for d in range(2):
        @pl.when(jnp.logical_not(has_z[d]))
        def _(d=d):
            ext[(0, bz + 1)[d]] = jnp.zeros(ext.shape[1:], ext.dtype)

        @pl.when(jnp.logical_not(has_y[d]))
        def _(d=d):
            for z in range(bz + 2):
                ext[z, (0, by + 1)[d]] = jnp.zeros(ext.shape[2:], ext.dtype)

    own.wait()
    blocks = [col] + [lax.rem(col + nc - j, nc) for j in range(1, nc)]
    for j, block in enumerate(blocks):
        order = [0] + [z for z in range(bz) if z > 0]
        for z in order:
            if j > 0:
                col_copy(j, z, block, (gz, gy, block)).wait_recv()
            if z == 0:
                pl.when(has_z[0])(lambda j=j, block=block: z_copy(j, block, 0).start())
            if z == bz - 1:
                pl.when(has_z[1])(lambda j=j, block=block: z_copy(j, block, 1).start())
        for d in range(2):
            pl.when(has_y[d])(lambda j=j, block=block, d=d: y_copy(j, block, d, 0).start())
    for j, block in enumerate(blocks):
        for h in range(2):
            @pl.when(has_z[h])
            def _(j=j, block=block, h=h):
                z_copy(j, block, 1 - h).wait_recv()
                for d in range(2):
                    pl.when(has_y[d])(lambda: y_copy(j, block, d, 1 + h).start())
    for j, block in enumerate(blocks):
        if j > 0:
            for z in range(bz):
                col_copy(j, z, block, (gz, gy, block)).wait_send()
        for d in range(2):
            pl.when(has_z[d])(lambda j=j, block=block, d=d: z_copy(j, block, d).wait_send())

            @pl.when(has_y[d])
            def _(j=j, block=block, d=d):
                y_copy(j, block, d, 0).wait_send()
                y_copy(j, block, 1 - d, 0).wait_recv()
                for h in range(2):
                    @pl.when(has_z[h])
                    def _(h=h):
                        y_copy(j, block, d, 1 + h).wait_send()
                        y_copy(j, block, 1 - d, 1 + h).wait_recv()


def gathered_brick(volume):
    bz, by, ch, bx = volume.shape
    nc = lax.axis_size("col")
    dma = pltpu.SemaphoreType.DMA
    return pl.pallas_call(
        gather_kernel,
        out_shape=jax.ShapeDtypeStruct((bz + 2, by + 2, nc, ch, bx), volume.dtype),
        in_specs=[pl.BlockSpec(memory_space=pl.ANY)],
        out_specs=VMEM,
        scratch_shapes=[
            dma, dma((nc, bz)), dma((nc, bz)), dma((nc, 2)), dma((nc, 2)),
            dma((nc, 2, 3)), dma((nc, 2, 3)),
        ],
        compiler_params=pltpu.CompilerParams(
            collective_id=0, has_side_effects=True, vmem_limit_bytes=32 << 20
        ),
        name="gather_brick",
    )(volume)


def conv_kernel(ext, weights, out, total):
    step_index = pl.program_id(0)
    dz, dx = step_index // 3, lax.rem(step_index, 3)
    bz, by, bx, wide = out.shape
    channels = weights.shape[-1]

    @pl.when(dz == 0)
    def _():
        total[dx] = jnp.zeros(total.shape[1:], total.dtype)

    for dy in range(3):
        cells = jnp.concatenate(
            [
                ext[dz + z, dy + y].reshape(channels, bx)
                for z in range(bz)
                for y in range(by)
            ],
            axis=1,
        )
        matrix = weights[0, dy, 0].reshape(2 * wide, channels)
        total[dx] += jnp.dot(matrix, cells, preferred_element_type=jnp.float32)

    @pl.when(step_index == pl.num_programs(0) - 1)
    def _():
        step = min(wide, 128)
        lane = lax.broadcasted_iota(jnp.int32, (step, bx), 1)

        def summed(z, first, y):
            rows, xs = pl.ds(first, step), pl.ds((z * by + y) * bx, bx)
            before = pltpu.roll(total[0, rows, xs], 1, 1)
            after = pltpu.roll(total[2, rows, xs], bx - 1, 1)
            return (
                total[1, rows, xs]
                + jnp.where(lane == 0, 0.0, before)
                + jnp.where(lane == bx - 1, 0.0, after)
            )

        for z in range(bz):
            for y in range(by):
                for first in range(0, wide, step):
                    gate = summed(z, first, y)
                    value = summed(z, wide + first, y)
                    gated = gate / (1.0 + jnp.exp(-gate)) * value
                    out[z, y, :, pl.ds(first, step)] = gated.T.astype(out.dtype)


def gated_conv(ext, weights, brick):
    bz, by = brick
    taps, two, wide, channels = weights.shape
    bx = ext.shape[-1]
    return pl.pallas_call(
        conv_kernel,
        grid=(9,),
        out_shape=jax.ShapeDtypeStruct((bz, by, bx, wide), jnp.bfloat16),
        in_specs=[
            pl.BlockSpec(ext.shape, lambda t: (0,) * 5),
            pl.BlockSpec(
                (1, 3, 1, two, wide, channels), lambda t: (t // 3, 0, t % 3, 0, 0, 0)
            ),
        ],
        out_specs=pl.BlockSpec((bz, by, bx, wide), lambda t: (0,) * 4),
        scratch_shapes=[pltpu.VMEM((3, two * wide, bz * by * bx), jnp.float32)],
        compiler_params=pltpu.CompilerParams(vmem_limit_bytes=48 << 20),
        cost_estimate=pl.CostEstimate(
            flops=2 * taps * two * wide * channels * bz * by * bx,
            bytes_accessed=2 * weights.size + 2 * ext.size,
            transcendentals=bz * by * bx * wide,
        ),
        name="gated_conv",
    )(ext, weights.reshape((3, 3, 3) + weights.shape[1:]))


def project_kernel(gated, proj, ext, other, rows, cs, cr, zs, zr, ys, yr):
    (gz, gy, col), (nz, ny, nc) = place()
    bz, by, bx, wide = gated.shape
    piece = bx // nc
    z_dev = ((lax.rem(gz + nz - 1, nz), gy, col), (lax.rem(gz + 1, nz), gy, col))
    y_dev = ((gz, lax.rem(gy + ny - 1, ny), col), (gz, lax.rem(gy + 1, ny), col))
    for j in range(1, nc):
        greet((gz, gy, lax.rem(col + j, nc)))
    for d in range(2):
        greet(z_dev[d])
        greet(y_dev[d])
    pl.semaphore_wait(pltpu.get_barrier_semaphore(), nc + 3)

    def col_copy(j, z):
        target = lax.rem(col + j, nc)
        xs = pl.ds(pl.multiple_of(target * piece, piece), piece)
        return remote(
            gated.at[z, :, xs], other.at[j, z], cs.at[j, z], cr.at[j, z], (gz, gy, target)
        )

    for z in range(bz):
        for j in range(1, nc):
            col_copy(j, z).start()

    def projected(cells, block):
        return jnp.dot(
            cells.reshape(by * piece, wide),
            proj[pl.ds(pl.multiple_of(block * wide, wide), wide), :],
            preferred_element_type=jnp.float32,
        )

    bands, quads, lanes = 4, piece // 4, ext.shape[-1]
    width = lanes // 4
    slot = lax.broadcasted_iota(jnp.int32, (quads, lanes), 1) // width
    def moves(n):
        return ((n, 0, True, 1), (n + 1, 1, False, 1), (2, n + 2, False, 0))

    def band(high):
        return pl.ds(1, 1) if high else pl.ds(0, 2)

    def z_copy(k):
        src, dst, high, d = moves(bz)[k]
        inner = pl.ds(2, by)
        return remote(
            ext.at[src, inner, band(high)], ext.at[dst, inner, band(high)],
            zs.at[k], zr.at[k], z_dev[d],
        )

    groups = ((2, bz, False), (0, 1, True), (1, 1, False), (bz + 2, 1, False))

    def y_copy(k, g):
        src, dst, high, d = moves(by)[k]
        start, size, z_high = groups[g]
        zr_ = pl.ds(start, size)
        return remote(
            ext.at[zr_, src, band(z_high), band(high)],
            ext.at[zr_, dst, band(z_high), band(high)],
            ys.at[k, g], yr.at[k, g], y_dev[d],
        )

    for z in range(bz):
        xs = pl.ds(pl.multiple_of(col * piece, piece), piece)
        total = projected(gated[z, :, xs, :], col)
        for j in range(1, nc):
            col_copy(j, z).wait_recv()
            total += projected(other[j, z], lax.rem(col + nc - j, nc))
        for b in range(4):
            rows[b, pl.ds(z * by * piece, by * piece), :] = total[:, b * lanes : (b + 1) * lanes]
        for y in range(by):
            first = (z * by + y) * piece
            for b in range(4):
                parts = [
                    rows[b, pl.ds(first + r, quads, stride=4), :]
                    for r in range(4)
                ]
                for q in range(bands):
                    packed = None
                    for r in range(4):
                        shift = ((r - q) * width) % lanes
                        part = pltpu.roll(parts[r], shift, 1) if shift else parts[r]
                        packed = part if packed is None else jnp.where(slot == r, part, packed)
                    ext[2 + z, 2 + y, b // 2, b % 2, q] = packed.astype(ext.dtype)
        for k in (1, 2, 0):
            if moves(bz)[k][0] == 2 + z:
                z_copy(k).start()

    for k in (1, 2, 0):
        y_copy(k, 0).start()
    for m in (1, 2, 0):
        z_copy(m).wait_recv()
        for k in (1, 2, 0):
            y_copy(k, m + 1).start()
    for j in range(1, nc):
        for z in range(bz):
            col_copy(j, z).wait_send()
    for k in range(3):
        z_copy(k).wait_send()
        for g in range(4):
            y_copy(k, g).wait_send()
    for k in range(3):
        for g in range(4):
            y_copy(k, g).wait_recv()


def projected_brick(gated, proj):
    bz, by, bx, wide = gated.shape
    nc = lax.axis_size("col")
    piece, lanes = bx // nc, proj.shape[1] // 4
    dma = pltpu.SemaphoreType.DMA
    return pl.pallas_call(
        project_kernel,
        out_shape=jax.ShapeDtypeStruct(
            (bz + 3, by + 3, 2, 2, 4, piece // 4, lanes), jnp.bfloat16
        ),
        in_specs=[VMEM, VMEM],
        out_specs=VMEM,
        scratch_shapes=[
            pltpu.VMEM((nc, bz, by, piece, wide), gated.dtype),
            pltpu.VMEM((4, bz * by * piece, lanes), jnp.float32),
            dma((nc, bz)), dma((nc, bz)), dma((3,)), dma((3,)), dma((3, 4)), dma((3, 4)),
        ],
        compiler_params=pltpu.CompilerParams(
            collective_id=1, has_side_effects=True, vmem_limit_bytes=32 << 20
        ),
        name="project",
    )(gated, proj)


def coarse_lift(low, high):
    count = len(high)
    even = [low[i] - 0.25 * (high[i - 1] + high[i]) for i in range(1, count)]
    odd = [high[i + 1] + 0.5 * (even[i] + even[i + 1]) for i in range(count - 2)]
    result = []
    for i in range(count - 2):
        result += [odd[i], even[i + 1]]
    return result


def fine_lift(low, high):
    count = len(high)
    even = [low[i] - 0.25 * (high[i - 1] + high[i]) for i in range(1, count)]
    result = []
    for i in range(count - 2):
        result += [even[i], high[i + 1] + 0.5 * (even[i] + even[i + 1])]
    return result


def synthesis_kernel(ext, out, middle, tiles):
    nz, ny = ext.shape[:2]
    for band in range(4):
        def column(y, hz, hy):
            return [
                None if z == 0 and not hz else ext[z, y, hz, hy, band].astype(jnp.float32)
                for z in range(nz)
            ]

        low = [
            None if y == 0 else coarse_lift(column(y, 0, 0), column(y, 1, 0))
            for y in range(ny)
        ]
        high = [coarse_lift(column(y, 0, 1), column(y, 1, 1)) for y in range(ny)]
        for z in range(len(high[0])):
            line = coarse_lift(
                [None if part is None else part[z] for part in low],
                [part[z] for part in high],
            )
            for y, cells in enumerate(line):
                middle[band, z, y] = cells
    mz, my = middle.shape[1:3]
    low, high = [], []
    for y in range(my):
        low.append(fine_lift([middle[0, z, y] for z in range(mz)], [middle[2, z, y] for z in range(mz)]))
        high.append(fine_lift([middle[1, z, y] for z in range(mz)], [middle[3, z, y] for z in range(mz)]))
    quads, lanes = middle.shape[3:]
    for z in range(out.shape[0]):
        line = fine_lift([part[z] for part in low], [part[z] for part in high])
        for y, cells in enumerate(line):
            tiles[z, pl.ds(y * quads, quads), :] = cells
        for quad in range(quads):
            out[z, :, pl.ds(quad * lanes, lanes)] = tiles[z, pl.ds(quad, out.shape[1], stride=quads), :]


def synthesized(ext):
    nz, ny = ext.shape[:2]
    quads, lanes = ext.shape[-2:]
    fz, fy = 4 * (nz - 3), 4 * (ny - 3)
    return pl.pallas_call(
        synthesis_kernel,
        out_shape=jax.ShapeDtypeStruct((fz, fy, quads * lanes), jnp.float32),
        in_specs=[VMEM],
        out_specs=VMEM,
        scratch_shapes=[
            pltpu.VMEM((4, 2 * (nz - 2), 2 * (ny - 2), quads, lanes), jnp.float32),
            pltpu.VMEM((fz, fy * quads, lanes), jnp.float32),
        ],
        compiler_params=pltpu.CompilerParams(vmem_limit_bytes=32 << 20),
        name="synthesis",
    )(ext)


def on_device_kernels(volume, conv_weight, proj_weight):
    ext = gathered_brick(volume)
    gated = gated_conv(ext, conv_weight, volume.shape[:2])
    return synthesized(projected_brick(gated, proj_weight))


def fits(volume, conv_weight, proj_weight):
    bz, by, ch, bx = volume.shape
    wide, piece = conv_weight.shape[2], bx // lax.axis_size("col")
    return (
        min(bz, by) >= 2
        and min(lax.axis_size("gz"), lax.axis_size("gy")) >= 3
        and ch % 16 == 0 and bx == 128 and wide % 128 == 0
        and piece % 64 == 0 and proj_weight.shape[1] == 4 * 128
    )


def extended_2(cells, sides, width, closed):
    for axis, dim in sides:
        count = lax.axis_size(axis)
        ends = count if closed else count - 1
        head = lax.slice_in_dim(cells, 0, width, axis=dim)
        tail = lax.slice_in_dim(cells, cells.shape[dim] - width, cells.shape[dim], axis=dim)
        cells = jnp.concatenate(
            [
                lax.ppermute(tail, axis, [(i, (i + 1) % count) for i in range(ends)]),
                cells,
                lax.ppermute(head, axis, [((i + 1) % count, i) for i in range(ends)]),
            ],
            axis=dim,
        )
    return cells


def inverse_lift(low_band, high_band, along):
    length = low_band.shape[along]

    def window_of(array, first, last):
        return lax.slice_in_dim(array, first, last, axis=along)

    even_rows = window_of(low_band, 1, length - 1) - 0.25 * (
        window_of(high_band, 0, length - 2) + window_of(high_band, 1, length - 1)
    )
    next_even = window_of(low_band, 2, length) - 0.25 * (
        window_of(high_band, 1, length - 1) + window_of(high_band, 2, length)
    )
    odd_rows = window_of(high_band, 1, length - 1) + 0.5 * (even_rows + next_even)
    paired = jnp.stack([even_rows, odd_rows], axis=along + 1)
    new_shape = list(even_rows.shape)
    new_shape[along] = 2 * (length - 2)
    return paired.reshape(new_shape)


def synthesize(coefficients):
    quarter = coefficients.shape[-1] // 4
    bands = coefficients.reshape(coefficients.shape[:-1] + (4, quarter))
    low_z = inverse_lift(bands[..., 0, :], bands[..., 2, :], 0)
    high_z = inverse_lift(bands[..., 1, :], bands[..., 3, :], 0)
    return inverse_lift(low_z, high_z, 1)


def convolve(brick_data, tap_weights):
    kernel = tap_weights.reshape(
        (3, 3, 3, tap_weights.shape[1] * tap_weights.shape[2], tap_weights.shape[3])
    )
    result = lax.conv_general_dilated(
        brick_data[None],
        kernel,
        (1, 1, 1),
        ((0, 0), (0, 0), (1, 1)),
        dimension_numbers=("NDHCW", "DHWOI", "NDHCW"),
        preferred_element_type=jnp.float32,
    )
    return result[0]


def on_device(volume, conv_weight, proj_weight):
    if fits(volume, conv_weight, proj_weight):
        return on_device_kernels(volume, conv_weight, proj_weight)
    out_width = conv_weight.shape[2]
    gathered = lax.all_gather(volume, "col", axis=2, tiled=True)
    extended = extended_2(gathered, (("gz", 0), ("gy", 1)), 1, False)
    conv_out = convolve(extended, conv_weight)
    gated_values = (
        jax.nn.silu(conv_out[:, :, :out_width, :]) * conv_out[:, :, out_width:, :]
    ).astype(jnp.bfloat16)
    coefficients = jnp.einsum(
        "zycx,cp->zyxp",
        lax.all_to_all(gated_values, "col", split_axis=3, concat_axis=2, tiled=True),
        proj_weight,
        preferred_element_type=jnp.float32,
    )
    coarse = extended_2(coefficients, (("gz", 0), ("gy", 1)), 1, True)
    middle = synthesize(coarse)
    middle_rims = extended_2(middle, (("gz", 0), ("gy", 1)), 1, True)
    fine_tiles = synthesize(middle_rims)
    return fine_tiles.reshape(
        (fine_tiles.shape[0], fine_tiles.shape[1], fine_tiles.shape[2] * fine_tiles.shape[3])
    )


def solution(mesh):
    return jax.shard_map(
        on_device,
        mesh=mesh,
        in_specs=(P("gz", "gy", "col", None), P(None, None, "col", None), P()),
        out_specs=P("gz", "gy", "col"),
        check_vma=False,
    )
```
